32 devices in a mesh: row: 8 (over y, x, core), col: 4 (over z).
Axes of the slice: x: 2, y: 2, z: 4, core: 2. Of those that a mesh axis runs over, the one named last changes fastest.
Arguments:
- ratings: bfloat16 [4, 65536, 512], P(None, ('row', 'col'))
- tile_mask: int32 [4, 512, 4], P(None, ('row', 'col')), may hold values from 0 to 1, as said below
- tile_counts: int32 [32], replicated, may hold values from 1 to 16, as said below
- users: float32 [32768, 128], P(('row', 'col')), may hold values from -2 to 2
- user_accum: float32 [32768, 128], P(('row', 'col')), may hold values from 0.05 to 0.5
- items: float32 [16384, 128], P(('row', 'col')), may hold values from -2 to 2
- item_accum: float32 [16384, 128], P(('row', 'col')), may hold values from 0.05 to 0.5
Outputs:
- users_out: float32 [32768, 128], P(('row', 'col'))
- user_accum_out: float32 [32768, 128], P(('row', 'col'))
- items_out: float32 [16384, 128], P(('row', 'col'))
- item_accum_out: float32 [16384, 128], P(('row', 'col'))
- losses: float32 [4], replicated
The draws below stay inside these ranges and needn't reach their ends.
Inputs may be any that keep to these rules, and one draw needn't show every extreme that they name: Each group of 4 positions has tile_counts summing to 32, and exactly one position of each group, not always the same, owns 2 * 8 tiles. `tile_mask`: in each stratum, the first slot's first item tile of every position is 1.
All inputs are finite; a program needn't handle non-finite values.
Results may differ from the reference program's by a relative error of at most 0.0025.
Values sent between devices are 32-bit elements; how exact they have to be, the bound alone decides.
A program may use at most 64 MiB of HBM per device.

```python
import math
import jax
import jax.numpy as jnp
from jax import lax

R = 128
TILE = 128
UT = 8
IT = 4
STRATA = 4
STEPS = 3
CAP = 16
GROUP = 4
LOOP = 32
USERS = 32768
ITEMS = 16384
N_ROW = 8
N_COL = 4


def draw_ratings(key, part):
    keys = jax.random.split(jax.random.fold_in(key, 11), 3)
    row_total = LOOP * CAP * TILE
    shape = (STRATA, row_total, IT * TILE)
    rise = 1.0 + 2.0 * jnp.arange(row_total, dtype=jnp.float32) / float(row_total)
    row_factor = jax.random.uniform(keys[1], (row_total,), jnp.float32, 0.6, 1.4)
    col_factor = jax.random.uniform(keys[2], (STRATA, 1, IT * TILE), jnp.float32, 0.6, 1.4)
    base = jax.random.normal(keys[0], shape, jnp.float32)
    values = base * (rise * row_factor)[None, :, None] * col_factor
    return values.astype(jnp.bfloat16)


def draw_tile_mask(key, part):
    keys = jax.random.split(jax.random.fold_in(key, 23), 2)
    level = jax.random.randint(keys[0], (STRATA, LOOP, 1, 1), 15, 95)
    rolled = jax.random.randint(keys[1], (STRATA, LOOP, CAP, IT), 0, 100)
    first = (jnp.arange(CAP)[:, None] == 0) & (jnp.arange(IT)[None, :] == 0)
    live_tiles = jnp.where(first[None, None], 1, (rolled < level).astype(jnp.int32))
    return live_tiles.reshape(STRATA, LOOP * CAP, IT).astype(jnp.int32)


def draw_tile_counts(key, part):
    keys = jax.random.split(jax.random.fold_in(key, 37), 2)
    group_count = LOOP // GROUP
    heavy = jax.random.randint(keys[0], (group_count, 1), 0, GROUP)
    pieces = jax.random.randint(keys[1], (group_count, 2), 1, UT)
    third = 2 * UT - pieces[:, 0:1] - pieces[:, 1:2]
    others = jnp.concatenate([pieces, third], axis=1)
    ranks = jnp.arange(GROUP, dtype=jnp.int32)[None, :]
    other_rank = jnp.clip(ranks - (ranks > heavy).astype(jnp.int32), 0, 2)
    picked = jnp.take_along_axis(others, other_rank, axis=1)
    values = jnp.where(ranks == heavy, 2 * UT, picked)
    return values.reshape(LOOP).astype(jnp.int32)


def block_scale(stream_key, dims, shards, least, top_value):
    factor_of, own = 1.0, jax.random.fold_in(stream_key, 6)
    for axis_at, shards_of in shards:
        heights = jnp.exp(jax.random.uniform(jax.random.fold_in(own, axis_at), (shards_of,), jnp.float32, least / len(shards), top_value / len(shards)))
        factor_of = factor_of * jnp.repeat(heights, dims[axis_at] // shards_of).reshape([-1 if axis == axis_at else 1 for axis in range(len(dims))])
    return factor_of


def normal_values(own_key, extent, deviation, reach, cuts=(), kind=jnp.bfloat16):
    array = deviation * jax.random.normal(own_key, extent, jnp.float32)
    if cuts:
        array = array * block_scale(own_key, extent, cuts, -0.22, 0.18)
    return jnp.clip(array, -reach, reach).astype(kind)


def setup_inputs(seed: int = 0) -> dict:
    key_list = jax.random.split(jax.random.key(seed), 8)
    ratings = draw_ratings(jax.random.fold_in(key_list[7], 71), 0)
    tile_mask = draw_tile_mask(jax.random.fold_in(key_list[7], 71), 0)
    tile_counts = draw_tile_counts(jax.random.fold_in(key_list[7], 71), 0)
    users = normal_values(key_list[3], (USERS, R), 0.3, 2.0, ((0, 32),), jnp.float32)
    user_accum = jnp.clip(jnp.exp(math.log(0.5) - 2.3025851 * jax.random.uniform(key_list[4], (USERS, R), jnp.float32) ** block_scale(key_list[4], (USERS, R), ((0, 32),), -0.2, 0.2)), 0.05, 0.5)
    items = normal_values(key_list[5], (ITEMS, R), 0.3, 2.0, ((0, 32),), jnp.float32)
    item_accum = jnp.clip(jnp.exp(math.log(0.5) - 2.3025851 * jax.random.uniform(key_list[6], (ITEMS, R), jnp.float32) ** block_scale(key_list[6], (ITEMS, R), ((0, 32),), -0.2, 0.2)), 0.05, 0.5)
    return dict(ratings=ratings, tile_mask=tile_mask, tile_counts=tile_counts, users=users, user_accum=user_accum, items=items, item_accum=item_accum)


ridge_weight = 0.02
step_rate = 0.05

def update(user_fac, user_acc, item_fac, item_acc, rating_block, live_tiles):
    tile_size = user_fac.shape[0] // live_tiles.shape[0]
    user_half = user_fac.astype(jnp.bfloat16)
    item_half = item_fac.astype(jnp.bfloat16)
    predicted = lax.dot_general(user_half, item_half, (((1,), (1,)), ((), ())), preferred_element_type=jnp.float32)
    residue = predicted - rating_block.astype(jnp.float32)
    masked = (residue.reshape(live_tiles.shape[0], tile_size, live_tiles.shape[1], tile_size) * live_tiles[:, None, :, None]).reshape(residue.shape)
    sq_error = jnp.sum(masked * residue)
    err_half = masked.astype(jnp.bfloat16)
    grad_user = jnp.dot(err_half, item_half, preferred_element_type=jnp.float32) * float(item_fac.shape[0]) ** (-0.5) + ridge_weight * user_fac
    grad_item = lax.dot_general(err_half, user_half, (((0,), (0,)), ((), ())), preferred_element_type=jnp.float32) * float(UT * TILE) ** (-0.5) + ridge_weight * item_fac
    user_acc = user_acc + grad_user * grad_user
    item_acc = item_acc + grad_item * grad_item
    user_fac = user_fac - step_rate * grad_user * lax.rsqrt(user_acc)
    item_fac = item_fac - step_rate * grad_item * lax.rsqrt(item_acc)
    return (user_fac, user_acc, item_fac, item_acc, sq_error)

def apply_update(packed):
    return update(packed[0], packed[1], packed[2], packed[3], packed[4], packed[5])

def reference(ratings, tile_mask, tile_counts, users, user_accum, items, item_accum):
    loop_len = N_ROW * N_COL
    slot_count = 2 * UT
    group_tiles = N_COL * UT
    item_rows = IT * TILE
    count_grid = tile_counts.reshape(N_ROW, N_COL)
    starts = (jnp.cumsum(count_grid, axis=1) - count_grid).reshape(loop_len).astype(jnp.int32)
    offsets = jnp.arange(slot_count, dtype=jnp.int32)
    local = (starts[:, None] + offsets[None, :]) % group_tiles
    group_base = jnp.arange(loop_len, dtype=jnp.int32) // N_COL * group_tiles
    tile_index = (group_base[:, None] + local).astype(jnp.int32)
    valid = offsets[None, :] < tile_counts[:, None]
    user_tiles = users.reshape(-1, TILE, R)
    acc_tiles = user_accum.reshape(-1, TILE, R)
    user_fac = user_tiles[tile_index].reshape(loop_len, slot_count * TILE, R)
    user_acc = acc_tiles[tile_index].reshape(loop_len, slot_count * TILE, R)
    item_fac = items.reshape(loop_len, item_rows, R)
    item_acc = item_accum.reshape(loop_len, item_rows, R)
    live_all = tile_mask.reshape(STRATA, loop_len, slot_count, IT).astype(jnp.float32) * valid.astype(jnp.float32)[None, :, :, None]
    rating_all = ratings.reshape(STRATA, loop_len, slot_count * TILE, item_rows)
    loss_list = []
    for stratum in range(STRATA):
        for inner in range(STEPS):
            user_fac, user_acc, item_fac, item_acc, sq_error = lax.map(apply_update, (user_fac, user_acc, item_fac, item_acc, rating_all[stratum], live_all[stratum]))
            if inner == 0:
                loss_list.append(jnp.sum(sq_error) / (jnp.sum(live_all[stratum]) * float(TILE * TILE)))
        if stratum + 1 < STRATA:
            item_fac = jnp.roll(item_fac, 1, 0)
            item_acc = jnp.roll(item_acc, 1, 0)
    total_tiles = USERS // TILE
    target = jnp.where(valid, tile_index, total_tiles).reshape(-1).astype(jnp.int32)
    users_new = jnp.zeros((total_tiles, TILE, R), user_fac.dtype).at[target].set(user_fac.reshape(-1, TILE, R), mode='drop')
    accum_new = jnp.zeros((total_tiles, TILE, R), user_acc.dtype).at[target].set(user_acc.reshape(-1, TILE, R), mode='drop')
    return (users_new.reshape(-1, R), accum_new.reshape(-1, R), item_fac.reshape(-1, R), item_acc.reshape(-1, R), jnp.stack(loss_list))
```

```python
import jax
import jax.numpy as jnp
from jax import lax
from jax.sharding import PartitionSpec as P

TILE = 128
UT = 8
STEPS = 3


ridge_weight = 0.02
step_rate = 0.05


def passed_along(value, axis, steps):
    count = lax.axis_size(axis)
    pairs = [(source, (source + steps) % count) for source in range(count)]
    return lax.ppermute(value, axis, pairs)


def update(user_fac, user_acc, item_fac, item_acc, rating_block, live_tiles):
    tile_size = user_fac.shape[0] // live_tiles.shape[0]
    user_half = user_fac.astype(jnp.bfloat16)
    item_half = item_fac.astype(jnp.bfloat16)
    predicted = lax.dot_general(
        user_half, item_half, (((1,), (1,)), ((), ())), preferred_element_type=jnp.float32
    )
    residue = predicted - rating_block.astype(jnp.float32)
    masked = (
        residue.reshape(live_tiles.shape[0], tile_size, live_tiles.shape[1], tile_size)
        * live_tiles[:, None, :, None]
    ).reshape(residue.shape)
    sq_error = jnp.sum(masked * residue)
    err_half = masked.astype(jnp.bfloat16)
    grad_user = (
        jnp.dot(err_half, item_half, preferred_element_type=jnp.float32)
        * float(item_fac.shape[0]) ** (-0.5)
        + ridge_weight * user_fac
    )
    grad_item = (
        lax.dot_general(
            err_half, user_half, (((0,), (0,)), ((), ())), preferred_element_type=jnp.float32
        )
        * float(UT * TILE) ** (-0.5)
        + ridge_weight * item_fac
    )
    user_acc = user_acc + grad_user * grad_user
    item_acc = item_acc + grad_item * grad_item
    user_fac = user_fac - step_rate * grad_user * lax.rsqrt(user_acc)
    item_fac = item_fac - step_rate * grad_item * lax.rsqrt(item_acc)
    return (user_fac, user_acc, item_fac, item_acc, sq_error)


def segment_plan(group_size, own_tiles):
    total = group_size * own_tiles
    low = [m if m < group_size - 1 else total - 2 * own_tiles for m in range(group_size)]
    high = [total - (group_size - 1 - m) if m else 2 * own_tiles for m in range(group_size)]
    segments = []
    for step in range(1 - group_size, group_size):
        first, last, pairs = own_tiles, 0, []
        for m in range(group_size):
            home = m + step
            if 0 <= home < group_size:
                begin = max(low[m], home * own_tiles) - home * own_tiles
                end = min(high[m], (home + 1) * own_tiles) - home * own_tiles
                if begin < end:
                    first, last = min(first, begin), max(last, end)
                    pairs.append((home, m))
        if step == 0:
            first, last = 0, own_tiles
        if pairs:
            segments.append((step, first, last, pairs))
    return segments


def fetched(own, segments, tile_size, window, rows):
    parts = []
    for step, first, last, pairs in segments:
        part = own[first * tile_size : last * tile_size]
        parts.append(lax.ppermute(part, "col", pairs) if step else part)
    parts.append(jnp.zeros((rows, own.shape[1]), own.dtype))
    return lax.dynamic_slice_in_dim(jnp.concatenate(parts, axis=0), window, rows, 0)


def returned(kept, segments, tile_size, window):
    lengths = [(last - first) * tile_size for step, first, last, pairs in segments]
    frame = jnp.zeros((sum(lengths) + kept.shape[0], kept.shape[1]), kept.dtype)
    frame = lax.dynamic_update_slice_in_dim(frame, kept, window, 0)
    own_rows = [length for length, segment in zip(lengths, segments) if segment[0] == 0][0]
    total, at = None, 0
    for length, (step, first, last, pairs) in zip(lengths, segments):
        part = frame[at : at + length]
        at += length
        if step:
            part = lax.ppermute(part, "col", [(m, home) for home, m in pairs])
        part = jnp.pad(part, ((first * tile_size, own_rows - last * tile_size), (0, 0)))
        total = part if total is None else total + part
    return total


def on_device(ratings, tile_mask, tile_counts, users, user_accum, items, item_accum):
    strata_count = ratings.shape[0]
    slot_count = tile_mask.shape[1]
    tile_size = ratings.shape[1] // slot_count
    group_size = lax.axis_size("col")
    member = lax.axis_index("col")
    arrived_rows = users.shape[0]
    group_counts = lax.dynamic_slice_in_dim(
        tile_counts, lax.axis_index("row") * group_size, group_size
    )
    ranks = jnp.arange(group_size, dtype=jnp.int32)
    start_tile = jnp.sum(jnp.where(ranks < member, group_counts, 0))
    own_count = jnp.sum(jnp.where(ranks == member, group_counts, 0))
    valid = (jnp.arange(slot_count, dtype=jnp.int32) < own_count).astype(jnp.float32)
    pad_rows = slot_count * tile_size
    segments = segment_plan(group_size, arrived_rows // tile_size)
    ahead = -min(step * (arrived_rows // tile_size) + first for step, first, last, pairs in segments)
    window = (start_tile - member * (arrived_rows // tile_size) + ahead) * tile_size
    row_valid = jnp.repeat(valid, tile_size)[:, None] > 0.5
    user_fac = jnp.where(row_valid, fetched(users, segments, tile_size, window, pad_rows), 0.0)
    user_acc = jnp.where(row_valid, fetched(user_accum, segments, tile_size, window, pad_rows), 1.0)
    held_pair = jnp.stack([items, item_accum])
    loss_list = []
    for stratum in range(strata_count):
        live_tiles = tile_mask[stratum].astype(jnp.float32) * valid[:, None]
        item_fac = held_pair[0]
        item_acc = held_pair[1]
        for inner in range(STEPS):
            user_fac, user_acc, item_fac, item_acc, sq_error = update(
                user_fac, user_acc, item_fac, item_acc, ratings[stratum], live_tiles
            )
            if inner == 0:
                observed = jnp.sum(live_tiles) * float(tile_size * tile_size)
                total_error, total_count = lax.psum((sq_error, observed), ("row", "col"))
                loss_list.append(total_error / total_count)
        held_pair = jnp.stack([item_fac, item_acc])
        if stratum + 1 < strata_count:
            held_pair = passed_along(held_pair, ("row", "col"), 1)
    losses = jnp.stack(loss_list)
    users_new = returned(jnp.where(row_valid, user_fac, 0.0), segments, tile_size, window)
    accum_new = returned(jnp.where(row_valid, user_acc, 0.0), segments, tile_size, window)
    return (users_new, accum_new, held_pair[0], held_pair[1], losses)


def solution(mesh):
    return jax.shard_map(
        on_device,
        mesh=mesh,
        in_specs=(
            P(None, ("row", "col"), None),
            P(None, ("row", "col"), None),
            P(),
            P(("row", "col"), None),
            P(("row", "col"), None),
            P(("row", "col"), None),
            P(("row", "col"), None),
        ),
        out_specs=(
            P(("row", "col"), None),
            P(("row", "col"), None),
            P(("row", "col"), None),
            P(("row", "col"), None),
            P(),
        ),
        check_vma=False,
    )
```

```python
import functools

import jax
import jax.numpy as jnp
from jax import lax
from jax.experimental import pallas as pl
from jax.experimental.pallas import tpu as pltpu
from jax.sharding import PartitionSpec as P

TILE = 128
UT = 8
STEPS = 3


ridge_weight = 0.02
step_rate = 0.05


def passed_along(value, axis, steps):
    count = lax.axis_size(axis)
    pairs = [(source, (source + steps) % count) for source in range(count)]
    return lax.ppermute(value, axis, pairs)


def stratum_kernel(
    stratum, steps, chunks, user_scale, item_scale,
    count_ref, live_ref, ratings_hbm, fac_in, acc_in, item_in, item_acc_in,
    fac, acc, item, item_acc, loss_ref,
    rating, err, item_half, item_grad, sq_sum, sems,
):
    slots, item_tiles = live_ref.shape
    rows = fac.shape[0] // chunks
    tile = fac.shape[0] // slots
    width = item.shape[0] // item_tiles
    per_chunk = slots // chunks

    def rating_copy(i):
        at = pl.ds(i * rows, rows)
        return pltpu.make_async_copy(ratings_hbm.at[stratum, at], rating.at[at], sems.at[i])

    for i in range(chunks):
        rating_copy(i).start()
    used = (count_ref[0] + per_chunk - 1) // per_chunk
    sq_sum[...] = jnp.zeros_like(sq_sum)
    for i in range(chunks):
        rating_copy(i).wait()

    def one_step(first):
        half = (item_in if first else item)[...].astype(jnp.bfloat16)
        item_half[...] = half
        item_grad[...] = jnp.zeros_like(item_grad)

        def chunk(i, carry):
            at = pl.ds(pl.multiple_of(i * rows, rows), rows)
            user = (fac_in if first else fac)[at]
            user_half = user.astype(jnp.bfloat16)
            predicted = lax.dot_general(
                user_half, item_half[...], (((1,), (1,)), ((), ())), preferred_element_type=jnp.float32
            )
            squares = None
            for t in range(per_chunk):
                for j in range(item_tiles):
                    block = pl.ds(pl.multiple_of(i * rows + t * tile, tile), tile)
                    cols = slice(j * width, (j + 1) * width)
                    diff = predicted[t * tile : (t + 1) * tile, cols] - rating[block, cols].astype(jnp.float32)
                    masked = diff * live_ref[i * per_chunk + t, j]
                    err[t * tile : (t + 1) * tile, cols] = masked.astype(jnp.bfloat16)
                    if first:
                        part = jnp.sum((masked * diff).reshape(-1, 8, width), axis=0)
                        squares = part if squares is None else squares + part
            if first:
                sq_sum[...] += squares
            grad = (
                jnp.dot(err[...], item_half[...], preferred_element_type=jnp.float32) * user_scale
                + ridge_weight * user
            )
            item_grad[...] += grad_of_items(err[...], user_half)
            new_acc = (acc_in if first else acc)[at] + grad * grad
            acc[at] = new_acc
            fac[at] = user - step_rate * grad * lax.rsqrt(new_acc)
            return carry

        lax.fori_loop(0, used, chunk, 0)
        old = (item_in if first else item)[...]
        grad = summed_grad(item_grad[...]) * item_scale + ridge_weight * old
        new_acc = (item_acc_in if first else item_acc)[...] + grad * grad
        item_acc[...] = new_acc
        item[...] = old - step_rate * grad * lax.rsqrt(new_acc)

    for step in range(steps):
        one_step(step == 0)
    loss_ref[...] = sq_sum[...]


TURNED = True


def grad_of_items(err, user_half):
    pair = (user_half, err) if TURNED else (err, user_half)
    return lax.dot_general(*pair, (((0,), (0,)), ((), ())), preferred_element_type=jnp.float32)


def summed_grad(total):
    return total.T if TURNED else total


def run_stratum(stratum, count, live_tiles, ratings, user_fac, user_acc, item_fac, item_acc):
    slots = live_tiles.shape[0]
    user_rows, rank = user_fac.shape
    item_rows = item_fac.shape[0]
    chunks = CHUNKS
    vmem = pl.BlockSpec(memory_space=pltpu.VMEM)
    smem = pl.BlockSpec(memory_space=pltpu.SMEM)
    like = [jax.ShapeDtypeStruct(x.shape, x.dtype) for x in (user_fac, user_acc, item_fac, item_acc)]
    return pl.pallas_call(
        functools.partial(
            stratum_kernel, stratum, STEPS, chunks,
            float(item_rows) ** (-0.5), float(UT * TILE) ** (-0.5),
        ),
        out_shape=like + [jax.ShapeDtypeStruct((8, item_rows // live_tiles.shape[1]), jnp.float32)],
        in_specs=[smem, smem, pl.BlockSpec(memory_space=pl.ANY)] + [vmem] * 4,
        out_specs=[vmem] * 5,
        scratch_shapes=[
            pltpu.VMEM((user_rows, item_rows), jnp.bfloat16),
            pltpu.VMEM((user_rows // chunks, item_rows), jnp.bfloat16),
            pltpu.VMEM((item_rows, rank), jnp.bfloat16),
            pltpu.VMEM((rank, item_rows) if TURNED else (item_rows, rank), jnp.float32),
            pltpu.VMEM((8, item_rows // live_tiles.shape[1]), jnp.float32),
            pltpu.SemaphoreType.DMA((chunks,)),
        ],
        compiler_params=pltpu.CompilerParams(vmem_limit_bytes=32 * 1024 * 1024),
    )(count, live_tiles, ratings, user_fac, user_acc, item_fac, item_acc)


CHUNKS = 4


def segment_plan(group_size, own_tiles):
    total = group_size * own_tiles
    low = [m if m < group_size - 1 else total - 2 * own_tiles for m in range(group_size)]
    high = [total - (group_size - 1 - m) if m else 2 * own_tiles for m in range(group_size)]
    segments = []
    for step in range(1 - group_size, group_size):
        first, last, pairs = own_tiles, 0, []
        for m in range(group_size):
            home = m + step
            if 0 <= home < group_size:
                begin = max(low[m], home * own_tiles) - home * own_tiles
                end = min(high[m], (home + 1) * own_tiles) - home * own_tiles
                if begin < end:
                    first, last = min(first, begin), max(last, end)
                    pairs.append((home, m))
        if step == 0:
            first, last = 0, own_tiles
        if pairs:
            segments.append((step, first, last, pairs))
    return segments


def fetched(own, segments, tile_size, window, rows):
    parts = []
    for step, first, last, pairs in segments:
        part = own[first * tile_size : last * tile_size]
        parts.append(lax.ppermute(part, "col", pairs) if step else part)
    parts.append(jnp.zeros((rows, own.shape[1]), own.dtype))
    return lax.dynamic_slice_in_dim(jnp.concatenate(parts, axis=0), window, rows, 0)


def returned(kept, segments, tile_size, window):
    lengths = [(last - first) * tile_size for step, first, last, pairs in segments]
    frame = jnp.zeros((sum(lengths) + kept.shape[0], kept.shape[1]), kept.dtype)
    frame = lax.dynamic_update_slice_in_dim(frame, kept, window, 0)
    own_rows = [length for length, segment in zip(lengths, segments) if segment[0] == 0][0]
    total, at = None, 0
    for length, (step, first, last, pairs) in zip(lengths, segments):
        part = frame[at : at + length]
        at += length
        if step:
            part = lax.ppermute(part, "col", [(m, home) for home, m in pairs])
        part = jnp.pad(part, ((first * tile_size, own_rows - last * tile_size), (0, 0)))
        total = part if total is None else total + part
    return total


def on_device(ratings, tile_mask, tile_counts, users, user_accum, items, item_accum):
    strata_count = ratings.shape[0]
    slot_count = tile_mask.shape[1]
    tile_size = ratings.shape[1] // slot_count
    group_size = lax.axis_size("col")
    member = lax.axis_index("col")
    arrived_rows = users.shape[0]
    group_counts = lax.dynamic_slice_in_dim(
        tile_counts, lax.axis_index("row") * group_size, group_size
    )
    ranks = jnp.arange(group_size, dtype=jnp.int32)
    start_tile = jnp.sum(jnp.where(ranks < member, group_counts, 0))
    own_count = jnp.sum(jnp.where(ranks == member, group_counts, 0))
    valid = (jnp.arange(slot_count, dtype=jnp.int32) < own_count).astype(jnp.float32)
    pad_rows = slot_count * tile_size
    segments = segment_plan(group_size, arrived_rows // tile_size)
    ahead = -min(step * (arrived_rows // tile_size) + first for step, first, last, pairs in segments)
    window = (start_tile - member * (arrived_rows // tile_size) + ahead) * tile_size
    row_valid = jnp.repeat(valid, tile_size)[:, None] > 0.5
    user_fac = jnp.where(row_valid, fetched(users, segments, tile_size, window, pad_rows), 0.0)
    user_acc = jnp.where(row_valid, fetched(user_accum, segments, tile_size, window, pad_rows), 1.0)
    item_fac, item_acc = items, item_accum
    live_all = tile_mask.astype(jnp.float32) * valid[:, None]
    sq_list = []
    for stratum in range(strata_count):
        user_fac, user_acc, item_fac, item_acc, squares = run_stratum(
            stratum, own_count[None], live_all[stratum], ratings, user_fac, user_acc, item_fac, item_acc
        )
        sq_list.append(jnp.sum(squares))
        if stratum + 1 < strata_count:
            item_fac = passed_along(item_fac, ("row", "col"), 1)
            item_acc = passed_along(item_acc, ("row", "col"), 1)
    observed = jnp.sum(live_all, axis=(1, 2)) * float(tile_size * tile_size)
    total_error, total_count = lax.psum((jnp.stack(sq_list), observed), ("row", "col"))
    losses = total_error / total_count
    users_new = returned(jnp.where(row_valid, user_fac, 0.0), segments, tile_size, window)
    accum_new = returned(jnp.where(row_valid, user_acc, 0.0), segments, tile_size, window)
    return (users_new, accum_new, item_fac, item_acc, losses)


def solution(mesh):
    return jax.shard_map(
        on_device,
        mesh=mesh,
        in_specs=(
            P(None, ("row", "col"), None),
            P(None, ("row", "col"), None),
            P(),
            P(("row", "col"), None),
            P(("row", "col"), None),
            P(("row", "col"), None),
            P(("row", "col"), None),
        ),
        out_specs=(
            P(("row", "col"), None),
            P(("row", "col"), None),
            P(("row", "col"), None),
            P(("row", "col"), None),
            P(),
        ),
        check_vma=False,
    )
```

```python
import functools

import jax
import jax.numpy as jnp
from jax import lax
from jax.experimental import pallas as pl
from jax.experimental.pallas import tpu as pltpu
from jax.sharding import PartitionSpec as P

TILE = 128
UT = 8
STEPS = 3


ridge_weight = 0.02
step_rate = 0.05


def passed_along(value, axis, steps):
    count = lax.axis_size(axis)
    pairs = [(source, (source + steps) % count) for source in range(count)]
    return lax.ppermute(value, axis, pairs)


def stratum_kernel(
    stratum, steps, chunks, user_scale, item_scale,
    count_ref, live_ref, ratings_hbm, fac_in, acc_in, pair_in,
    fac, acc, pair, loss_ref,
    rating, err, item_half, item_grad, sq_sum, sems,
):
    item_in, item_acc_in, item, item_acc = pair_in.at[0], pair_in.at[1], pair.at[0], pair.at[1]
    slots, item_tiles = live_ref.shape
    rows = fac.shape[0] // chunks
    tile = fac.shape[0] // slots
    width = item.shape[0] // item_tiles
    per_chunk = slots // chunks

    def rating_copy(i):
        at = pl.ds(i * rows, rows)
        return pltpu.make_async_copy(ratings_hbm.at[stratum, at], rating.at[at], sems.at[i])

    for i in range(chunks):
        rating_copy(i).start()
    used = (count_ref[0] + per_chunk - 1) // per_chunk
    sq_sum[...] = jnp.zeros_like(sq_sum)
    for i in range(chunks):
        rating_copy(i).wait()

    def one_step(first):
        half = (item_in if first else item)[...].astype(jnp.bfloat16)
        item_half[...] = half
        item_grad[...] = jnp.zeros_like(item_grad)

        def chunk(i, carry):
            at = pl.ds(pl.multiple_of(i * rows, rows), rows)
            user = (fac_in if first else fac)[at]
            user_half = user.astype(jnp.bfloat16)
            predicted = lax.dot_general(
                user_half, item_half[...], (((1,), (1,)), ((), ())), preferred_element_type=jnp.float32
            )
            squares = None
            for t in range(per_chunk):
                for j in range(item_tiles):
                    block = pl.ds(pl.multiple_of(i * rows + t * tile, tile), tile)
                    cols = slice(j * width, (j + 1) * width)
                    diff = predicted[t * tile : (t + 1) * tile, cols] - rating[block, cols].astype(jnp.float32)
                    masked = diff * live_ref[i * per_chunk + t, j]
                    err[t * tile : (t + 1) * tile, cols] = masked.astype(jnp.bfloat16)
                    if first:
                        part = jnp.sum((masked * diff).reshape(-1, 8, width), axis=0)
                        squares = part if squares is None else squares + part
            if first:
                sq_sum[...] += squares
            grad = (
                jnp.dot(err[...], item_half[...], preferred_element_type=jnp.float32) * user_scale
                + ridge_weight * user
            )
            item_grad[...] += grad_of_items(err[...], user_half)
            new_acc = (acc_in if first else acc)[at] + grad * grad
            acc[at] = new_acc
            fac[at] = user - step_rate * grad * lax.rsqrt(new_acc)
            return carry

        lax.fori_loop(0, used, chunk, 0)
        old = (item_in if first else item)[...]
        grad = summed_grad(item_grad[...]) * item_scale + ridge_weight * old
        new_acc = (item_acc_in if first else item_acc)[...] + grad * grad
        item_acc[...] = new_acc
        item[...] = old - step_rate * grad * lax.rsqrt(new_acc)

    for step in range(steps):
        one_step(step == 0)
    loss_ref[...] = sq_sum[...]


TURNED = True


def grad_of_items(err, user_half):
    pair = (user_half, err) if TURNED else (err, user_half)
    return lax.dot_general(*pair, (((0,), (0,)), ((), ())), preferred_element_type=jnp.float32)


def summed_grad(total):
    return total.T if TURNED else total


def run_stratum(stratum, count, live_tiles, ratings, user_fac, user_acc, held_pair):
    slots = live_tiles.shape[0]
    user_rows, rank = user_fac.shape
    item_rows = held_pair.shape[1]
    chunks = CHUNKS
    vmem = pl.BlockSpec(memory_space=pltpu.VMEM)
    smem = pl.BlockSpec(memory_space=pltpu.SMEM)
    like = [jax.ShapeDtypeStruct(x.shape, x.dtype) for x in (user_fac, user_acc, held_pair)]
    return pl.pallas_call(
        functools.partial(
            stratum_kernel, stratum, STEPS, chunks,
            float(item_rows) ** (-0.5), float(UT * TILE) ** (-0.5),
        ),
        out_shape=like + [jax.ShapeDtypeStruct((8, item_rows // live_tiles.shape[1]), jnp.float32)],
        in_specs=[smem, smem, pl.BlockSpec(memory_space=pl.ANY)] + [vmem] * 3,
        out_specs=[vmem] * 4,
        scratch_shapes=[
            pltpu.VMEM((user_rows, item_rows), jnp.bfloat16),
            pltpu.VMEM((user_rows // chunks, item_rows), jnp.bfloat16),
            pltpu.VMEM((item_rows, rank), jnp.bfloat16),
            pltpu.VMEM((rank, item_rows) if TURNED else (item_rows, rank), jnp.float32),
            pltpu.VMEM((8, item_rows // live_tiles.shape[1]), jnp.float32),
            pltpu.SemaphoreType.DMA((chunks,)),
        ],
        compiler_params=pltpu.CompilerParams(vmem_limit_bytes=52 * 1024 * 1024),
    )(count, live_tiles, ratings, user_fac, user_acc, held_pair)


CHUNKS = 4


def segment_plan(group_size, own_tiles):
    total = group_size * own_tiles
    low = [m if m < group_size - 1 else total - 2 * own_tiles for m in range(group_size)]
    high = [total - (group_size - 1 - m) if m else 2 * own_tiles for m in range(group_size)]
    segments = []
    for step in range(1 - group_size, group_size):
        first, last, pairs = own_tiles, 0, []
        for m in range(group_size):
            home = m + step
            if 0 <= home < group_size:
                begin = max(low[m], home * own_tiles) - home * own_tiles
                end = min(high[m], (home + 1) * own_tiles) - home * own_tiles
                if begin < end:
                    first, last = min(first, begin), max(last, end)
                    pairs.append((home, m))
        if step == 0:
            first, last = 0, own_tiles
        if pairs:
            segments.append((step, first, last, pairs))
    return segments


def fetched(own, segments, tile_size, window, rows):
    parts = []
    for step, first, last, pairs in segments:
        part = own[first * tile_size : last * tile_size]
        parts.append(lax.ppermute(part, "col", pairs) if step else part)
    parts.append(jnp.zeros((rows, own.shape[1]), own.dtype))
    return lax.dynamic_slice_in_dim(jnp.concatenate(parts, axis=0), window, rows, 0)


def returned(kept, segments, tile_size, window):
    lengths = [(last - first) * tile_size for step, first, last, pairs in segments]
    frame = jnp.zeros((sum(lengths) + kept.shape[0], kept.shape[1]), kept.dtype)
    frame = lax.dynamic_update_slice_in_dim(frame, kept, window, 0)
    own_rows = [length for length, segment in zip(lengths, segments) if segment[0] == 0][0]
    total, at = None, 0
    for length, (step, first, last, pairs) in zip(lengths, segments):
        part = frame[at : at + length]
        at += length
        if step:
            part = lax.ppermute(part, "col", [(m, home) for home, m in pairs])
        part = jnp.pad(part, ((first * tile_size, own_rows - last * tile_size), (0, 0)))
        total = part if total is None else total + part
    return total


def on_device(ratings, tile_mask, tile_counts, users, user_accum, items, item_accum):
    strata_count = ratings.shape[0]
    slot_count = tile_mask.shape[1]
    tile_size = ratings.shape[1] // slot_count
    group_size = lax.axis_size("col")
    member = lax.axis_index("col")
    arrived_rows = users.shape[0]
    group_counts = lax.dynamic_slice_in_dim(
        tile_counts, lax.axis_index("row") * group_size, group_size
    )
    ranks = jnp.arange(group_size, dtype=jnp.int32)
    start_tile = jnp.sum(jnp.where(ranks < member, group_counts, 0))
    own_count = jnp.sum(jnp.where(ranks == member, group_counts, 0))
    valid = (jnp.arange(slot_count, dtype=jnp.int32) < own_count).astype(jnp.float32)
    pad_rows = slot_count * tile_size
    segments = segment_plan(group_size, arrived_rows // tile_size)
    ahead = -min(step * (arrived_rows // tile_size) + first for step, first, last, pairs in segments)
    window = (start_tile - member * (arrived_rows // tile_size) + ahead) * tile_size
    row_valid = jnp.repeat(valid, tile_size)[:, None] > 0.5
    user_fac = jnp.where(row_valid, fetched(users, segments, tile_size, window, pad_rows), 0.0)
    user_acc = jnp.where(row_valid, fetched(user_accum, segments, tile_size, window, pad_rows), 1.0)
    held_pair = jnp.stack([items, item_accum])
    live_all = tile_mask.astype(jnp.float32) * valid[:, None]
    sq_list = []
    for stratum in range(strata_count):
        user_fac, user_acc, held_pair, squares = run_stratum(
            stratum, own_count[None], live_all[stratum], ratings, user_fac, user_acc, held_pair
        )
        sq_list.append(jnp.sum(squares))
        if stratum + 1 < strata_count:
            held_pair = passed_along(held_pair, ("row", "col"), 1)
    observed = jnp.sum(live_all, axis=(1, 2)) * float(tile_size * tile_size)
    total_error, total_count = lax.psum((jnp.stack(sq_list), observed), ("row", "col"))
    losses, user_fac, user_acc = lax.optimization_barrier((total_error / total_count, user_fac, user_acc))
    users_new = returned(jnp.where(row_valid, user_fac, 0.0), segments, tile_size, window)
    accum_new = returned(jnp.where(row_valid, user_acc, 0.0), segments, tile_size, window)
    return (users_new, accum_new, held_pair[0], held_pair[1], losses)


def solution(mesh):
    return jax.shard_map(
        on_device,
        mesh=mesh,
        in_specs=(
            P(None, ("row", "col"), None),
            P(None, ("row", "col"), None),
            P(),
            P(("row", "col"), None),
            P(("row", "col"), None),
            P(("row", "col"), None),
            P(("row", "col"), None),
        ),
        out_specs=(
            P(("row", "col"), None),
            P(("row", "col"), None),
            P(("row", "col"), None),
            P(("row", "col"), None),
            P(),
        ),
        check_vma=False,
    )
```

```python
import functools

import jax
import jax.numpy as jnp
from jax import lax
from jax.experimental import pallas as pl
from jax.experimental.pallas import tpu as pltpu
from jax.sharding import PartitionSpec as P

TILE = 128
UT = 8
STEPS = 3


ridge_weight = 0.02
step_rate = 0.05


def passed_along(value, axis, steps):
    count = lax.axis_size(axis)
    pairs = [(source, (source + steps) % count) for source in range(count)]
    return lax.ppermute(value, axis, pairs)


def stratum_kernel(
    stratum, steps, chunks, user_scale, item_scale,
    count_ref, live_ref, ratings_hbm, fac_in, acc_in, pair_in,
    fac, acc, pair, loss_ref,
    rating, err, item_half, item_grad, sq_sum, sems,
):
    item_in, item_acc_in, item, item_acc = pair_in.at[0], pair_in.at[1], pair.at[0], pair.at[1]
    slots, item_tiles = live_ref.shape
    rows = fac.shape[0] // chunks
    tile = fac.shape[0] // slots
    width = item.shape[0] // item_tiles
    per_chunk = slots // chunks

    def rating_copy(i):
        at = pl.ds(i * rows, rows)
        return pltpu.make_async_copy(ratings_hbm.at[stratum, at], rating.at[at], sems.at[i])

    for i in range(chunks):
        rating_copy(i).start()
    used = (count_ref[0] + per_chunk - 1) // per_chunk
    sq_sum[...] = jnp.zeros_like(sq_sum)
    for i in range(chunks):
        rating_copy(i).wait()

    def one_step(first):
        half = (item_in if first else item)[...].astype(jnp.bfloat16)
        item_half[...] = half
        item_grad[...] = jnp.zeros_like(item_grad)

        def chunk(i, carry):
            at = pl.ds(pl.multiple_of(i * rows, rows), rows)
            user = (fac_in if first else fac)[at]
            user_half = user.astype(jnp.bfloat16)
            predicted = lax.dot_general(
                user_half, item_half[...], (((1,), (1,)), ((), ())), preferred_element_type=jnp.float32
            )
            squares = None
            for t in range(per_chunk):
                for j in range(item_tiles):
                    block = pl.ds(pl.multiple_of(i * rows + t * tile, tile), tile)
                    cols = slice(j * width, (j + 1) * width)
                    diff = predicted[t * tile : (t + 1) * tile, cols] - rating[block, cols].astype(jnp.float32)
                    masked = diff * live_ref[i * per_chunk + t, j]
                    err[t * tile : (t + 1) * tile, cols] = masked.astype(jnp.bfloat16)
                    if first:
                        part = jnp.sum((masked * diff).reshape(-1, 8, width), axis=0)
                        squares = part if squares is None else squares + part
            if first:
                sq_sum[...] += squares
            grad = (
                jnp.dot(err[...], item_half[...], preferred_element_type=jnp.float32) * user_scale
                + ridge_weight * user
            )
            item_grad[...] += grad_of_items(err[...], user_half)
            new_acc = (acc_in if first else acc)[at] + grad * grad
            acc[at] = new_acc
            fac[at] = user - step_rate * grad * lax.rsqrt(new_acc)
            return carry

        lax.fori_loop(0, used, chunk, 0)
        old = (item_in if first else item)[...]
        grad = summed_grad(item_grad[...]) * item_scale + ridge_weight * old
        new_acc = (item_acc_in if first else item_acc)[...] + grad * grad
        item_acc[...] = new_acc
        item[...] = old - step_rate * grad * lax.rsqrt(new_acc)

    for step in range(steps):
        one_step(step == 0)
    loss_ref[...] = sq_sum[...]


TURNED = True


def grad_of_items(err, user_half):
    pair = (user_half, err) if TURNED else (err, user_half)
    return lax.dot_general(*pair, (((0,), (0,)), ((), ())), preferred_element_type=jnp.float32)


def summed_grad(total):
    return total.T if TURNED else total


def run_stratum(stratum, count, live_tiles, ratings, user_fac, user_acc, held_pair):
    slots = live_tiles.shape[0]
    user_rows, rank = user_fac.shape
    item_rows = held_pair.shape[1]
    chunks = CHUNKS
    vmem = pl.BlockSpec(memory_space=pltpu.VMEM)
    smem = pl.BlockSpec(memory_space=pltpu.SMEM)
    like = [jax.ShapeDtypeStruct(x.shape, x.dtype) for x in (user_fac, user_acc, held_pair)]
    return pl.pallas_call(
        functools.partial(
            stratum_kernel, stratum, STEPS, chunks,
            float(item_rows) ** (-0.5), float(UT * TILE) ** (-0.5),
        ),
        out_shape=like + [jax.ShapeDtypeStruct((8, item_rows // live_tiles.shape[1]), jnp.float32)],
        in_specs=[smem, smem, pl.BlockSpec(memory_space=pl.ANY)] + [vmem] * 3,
        out_specs=[vmem] * 4,
        scratch_shapes=[
            pltpu.VMEM((user_rows, item_rows), jnp.bfloat16),
            pltpu.VMEM((user_rows // chunks, item_rows), jnp.bfloat16),
            pltpu.VMEM((item_rows, rank), jnp.bfloat16),
            pltpu.VMEM((rank, item_rows) if TURNED else (item_rows, rank), jnp.float32),
            pltpu.VMEM((8, item_rows // live_tiles.shape[1]), jnp.float32),
            pltpu.SemaphoreType.DMA((chunks,)),
        ],
        compiler_params=pltpu.CompilerParams(vmem_limit_bytes=52 * 1024 * 1024),
    )(count, live_tiles, ratings, user_fac, user_acc, held_pair)


CHUNKS = 4


def sum_kernel(axes, x_ref, out_ref, *scratch):
    barrier = pltpu.get_barrier_semaphore()
    peers = 0
    for axis, count in axes:
        me = lax.axis_index(axis)
        for k in range(1, count):
            pl.semaphore_signal(
                barrier, inc=1, device_id={axis: lax.rem(me + k, count)}, device_id_type=pl.DeviceIdType.MESH
            )
        peers += count - 1
    pl.semaphore_wait(barrier, peers)
    value = x_ref[...]
    for (axis, count), at in zip(axes, range(0, len(scratch), 3)):
        slots, send_sems, recv_sems = scratch[at : at + 3]
        me = lax.axis_index(axis)
        slots[0] = value
        copies = []
        for k in range(1, count):
            copy = pltpu.make_async_remote_copy(
                src_ref=slots.at[0],
                dst_ref=slots.at[k],
                send_sem=send_sems.at[k],
                recv_sem=recv_sems.at[k],
                device_id={axis: lax.rem(me + k, count)},
                device_id_type=pl.DeviceIdType.MESH,
            )
            copy.start()
            copies.append(copy)
        for copy in copies:
            copy.wait()
        value = slots[me]
        for source in range(1, count):
            value = value + slots[lax.rem(me - source + count, count)]
    out_ref[...] = value


def summed_everywhere(sums):
    axes = [(axis, lax.axis_size(axis)) for axis in ("col", "row")]
    scratch = []
    for axis, count in axes:
        scratch += [
            pltpu.VMEM((count,) + sums.shape, sums.dtype),
            pltpu.SemaphoreType.DMA((count,)),
            pltpu.SemaphoreType.DMA((count,)),
        ]
    vmem = pl.BlockSpec(memory_space=pltpu.VMEM)
    return pl.pallas_call(
        functools.partial(sum_kernel, axes),
        out_shape=jax.ShapeDtypeStruct(sums.shape, sums.dtype),
        in_specs=[vmem],
        out_specs=vmem,
        scratch_shapes=scratch,
        compiler_params=pltpu.CompilerParams(collective_id=0, has_side_effects=True),
    )(sums)


def segment_plan(group_size, own_tiles):
    total = group_size * own_tiles
    low = [m if m < group_size - 1 else total - 2 * own_tiles for m in range(group_size)]
    high = [total - (group_size - 1 - m) if m else 2 * own_tiles for m in range(group_size)]
    segments = []
    for step in range(1 - group_size, group_size):
        first, last, pairs = own_tiles, 0, []
        for m in range(group_size):
            home = m + step
            if 0 <= home < group_size:
                begin = max(low[m], home * own_tiles) - home * own_tiles
                end = min(high[m], (home + 1) * own_tiles) - home * own_tiles
                if begin < end:
                    first, last = min(first, begin), max(last, end)
                    pairs.append((home, m))
        if step == 0:
            first, last = 0, own_tiles
        if pairs:
            segments.append((step, first, last, pairs))
    return segments


def fetched(own, segments, tile_size, window, rows):
    parts = []
    for step, first, last, pairs in segments:
        part = own[first * tile_size : last * tile_size]
        parts.append(lax.ppermute(part, "col", pairs) if step else part)
    parts.append(jnp.zeros((rows, own.shape[1]), own.dtype))
    return lax.dynamic_slice_in_dim(jnp.concatenate(parts, axis=0), window, rows, 0)


def returned(kept, segments, tile_size, window):
    lengths = [(last - first) * tile_size for step, first, last, pairs in segments]
    frame = jnp.zeros((sum(lengths) + kept.shape[0], kept.shape[1]), kept.dtype)
    frame = lax.dynamic_update_slice_in_dim(frame, kept, window, 0)
    own_rows = [length for length, segment in zip(lengths, segments) if segment[0] == 0][0]
    total, at = None, 0
    for length, (step, first, last, pairs) in zip(lengths, segments):
        part = frame[at : at + length]
        at += length
        if step:
            part = lax.ppermute(part, "col", [(m, home) for home, m in pairs])
        part = jnp.pad(part, ((first * tile_size, own_rows - last * tile_size), (0, 0)))
        total = part if total is None else total + part
    return total


def on_device(ratings, tile_mask, tile_counts, users, user_accum, items, item_accum):
    strata_count = ratings.shape[0]
    slot_count = tile_mask.shape[1]
    tile_size = ratings.shape[1] // slot_count
    group_size = lax.axis_size("col")
    member = lax.axis_index("col")
    arrived_rows = users.shape[0]
    group_counts = lax.dynamic_slice_in_dim(
        tile_counts, lax.axis_index("row") * group_size, group_size
    )
    ranks = jnp.arange(group_size, dtype=jnp.int32)
    start_tile = jnp.sum(jnp.where(ranks < member, group_counts, 0))
    own_count = jnp.sum(jnp.where(ranks == member, group_counts, 0))
    valid = (jnp.arange(slot_count, dtype=jnp.int32) < own_count).astype(jnp.float32)
    pad_rows = slot_count * tile_size
    segments = segment_plan(group_size, arrived_rows // tile_size)
    ahead = -min(step * (arrived_rows // tile_size) + first for step, first, last, pairs in segments)
    window = (start_tile - member * (arrived_rows // tile_size) + ahead) * tile_size
    row_valid = jnp.repeat(valid, tile_size)[:, None] > 0.5
    user_fac = jnp.where(row_valid, fetched(users, segments, tile_size, window, pad_rows), 0.0)
    user_acc = jnp.where(row_valid, fetched(user_accum, segments, tile_size, window, pad_rows), 1.0)
    held_pair = jnp.stack([items, item_accum])
    live_all = tile_mask.astype(jnp.float32) * valid[:, None]
    sq_list = []
    for stratum in range(strata_count):
        user_fac, user_acc, held_pair, squares = run_stratum(
            stratum, own_count[None], live_all[stratum], ratings, user_fac, user_acc, held_pair
        )
        sq_list.append(jnp.sum(squares))
        if stratum + 1 < strata_count:
            held_pair = passed_along(held_pair, ("row", "col"), 1)
    observed = jnp.sum(live_all, axis=(1, 2)) * float(tile_size * tile_size)
    sums = jnp.concatenate([jnp.stack(sq_list), observed])
    sums = jnp.broadcast_to(jnp.pad(sums, (0, items.shape[1] - sums.shape[0]))[None, :], (8, items.shape[1]))
    totals = summed_everywhere(sums)[0]
    total_error, total_count = totals[:strata_count], totals[strata_count : 2 * strata_count]
    losses, user_fac, user_acc = lax.optimization_barrier((total_error / total_count, user_fac, user_acc))
    users_new = returned(jnp.where(row_valid, user_fac, 0.0), segments, tile_size, window)
    accum_new = returned(jnp.where(row_valid, user_acc, 0.0), segments, tile_size, window)
    return (users_new, accum_new, held_pair[0], held_pair[1], losses)


def solution(mesh):
    return jax.shard_map(
        on_device,
        mesh=mesh,
        in_specs=(
            P(None, ("row", "col"), None),
            P(None, ("row", "col"), None),
            P(),
            P(("row", "col"), None),
            P(("row", "col"), None),
            P(("row", "col"), None),
            P(("row", "col"), None),
        ),
        out_specs=(
            P(("row", "col"), None),
            P(("row", "col"), None),
            P(("row", "col"), None),
            P(("row", "col"), None),
            P(),
        ),
        check_vma=False,
    )
```

```python
import functools

import jax
import jax.numpy as jnp
from jax import lax
from jax.experimental import pallas as pl
from jax.experimental.pallas import tpu as pltpu
from jax.sharding import PartitionSpec as P

TILE = 128
UT = 8
STEPS = 3


ridge_weight = 0.02
step_rate = 0.05


def passed_along(value, axis, steps):
    count = lax.axis_size(axis)
    pairs = [(source, (source + steps) % count) for source in range(count)]
    return lax.ppermute(value, axis, pairs)


def stratum_kernel(
    stratum, steps, chunks, user_scale, item_scale,
    count_ref, live_ref, ratings_hbm, fac_in, acc_in, pair_in,
    fac, acc, pair, loss_ref,
    rating, err, item_half, item_grad, sq_sum, sems,
):
    item_in, item_acc_in, item, item_acc = pair_in.at[0], pair_in.at[1], pair.at[0], pair.at[1]
    slots, item_tiles = live_ref.shape
    rows = fac.shape[0] // chunks
    tile = fac.shape[0] // slots
    width = item.shape[0] // item_tiles
    per_chunk = slots // chunks

    def rating_copy(i):
        at = pl.ds(i * rows, rows)
        return pltpu.make_async_copy(ratings_hbm.at[stratum, at], rating.at[at], sems.at[i])

    for i in range(chunks):
        rating_copy(i).start()
    used = (count_ref[0] + per_chunk - 1) // per_chunk
    sq_sum[...] = jnp.zeros_like(sq_sum)
    for i in range(chunks):
        rating_copy(i).wait()

    def one_step(first):
        half = (item_in if first else item)[...].astype(jnp.bfloat16)
        item_half[...] = half
        item_grad[...] = jnp.zeros_like(item_grad)

        def chunk(i, carry):
            at = pl.ds(pl.multiple_of(i * rows, rows), rows)
            user = (fac_in if first else fac)[at]
            user_half = user.astype(jnp.bfloat16)
            predicted = lax.dot_general(
                user_half, item_half[...], (((1,), (1,)), ((), ())), preferred_element_type=jnp.float32
            )
            squares = None
            for t in range(per_chunk):
                for j in range(item_tiles):
                    block = pl.ds(pl.multiple_of(i * rows + t * tile, tile), tile)
                    cols = slice(j * width, (j + 1) * width)
                    diff = predicted[t * tile : (t + 1) * tile, cols] - rating[block, cols].astype(jnp.float32)
                    masked = diff * live_ref[i * per_chunk + t, j]
                    err[t * tile : (t + 1) * tile, cols] = masked.astype(jnp.bfloat16)
                    if first:
                        part = jnp.sum((masked * diff).reshape(-1, 8, width), axis=0)
                        squares = part if squares is None else squares + part
            if first:
                sq_sum[...] += squares
            grad = (
                jnp.dot(err[...], item_half[...], preferred_element_type=jnp.float32) * user_scale
                + ridge_weight * user
            )
            item_grad[...] += grad_of_items(err[...], user_half)
            new_acc = (acc_in if first else acc)[at] + grad * grad
            acc[at] = new_acc
            fac[at] = user - step_rate * grad * lax.rsqrt(new_acc)
            return carry

        lax.fori_loop(0, used, chunk, 0)
        old = (item_in if first else item)[...]
        grad = summed_grad(item_grad[...]) * item_scale + ridge_weight * old
        new_acc = (item_acc_in if first else item_acc)[...] + grad * grad
        item_acc[...] = new_acc
        item[...] = old - step_rate * grad * lax.rsqrt(new_acc)

    for step in range(steps):
        one_step(step == 0)
    loss_ref[...] = sq_sum[...]


TURNED = True


def grad_of_items(err, user_half):
    pair = (user_half, err) if TURNED else (err, user_half)
    return lax.dot_general(*pair, (((0,), (0,)), ((), ())), preferred_element_type=jnp.float32)


def summed_grad(total):
    return total.T if TURNED else total


def run_stratum(stratum, count, live_tiles, ratings, user_fac, user_acc, held_pair):
    slots = live_tiles.shape[0]
    user_rows, rank = user_fac.shape
    item_rows = held_pair.shape[1]
    chunks = CHUNKS
    vmem = pl.BlockSpec(memory_space=pltpu.VMEM)
    smem = pl.BlockSpec(memory_space=pltpu.SMEM)
    like = [jax.ShapeDtypeStruct(x.shape, x.dtype) for x in (user_fac, user_acc, held_pair)]
    return pl.pallas_call(
        functools.partial(
            stratum_kernel, stratum, STEPS, chunks,
            float(item_rows) ** (-0.5), float(UT * TILE) ** (-0.5),
        ),
        out_shape=like + [jax.ShapeDtypeStruct((8, item_rows // live_tiles.shape[1]), jnp.float32)],
        in_specs=[smem, smem, pl.BlockSpec(memory_space=pl.ANY)] + [vmem] * 3,
        out_specs=[vmem] * 4,
        scratch_shapes=[
            pltpu.VMEM((user_rows, item_rows), jnp.bfloat16),
            pltpu.VMEM((user_rows // chunks, item_rows), jnp.bfloat16),
            pltpu.VMEM((item_rows, rank), jnp.bfloat16),
            pltpu.VMEM((rank, item_rows) if TURNED else (item_rows, rank), jnp.float32),
            pltpu.VMEM((8, item_rows // live_tiles.shape[1]), jnp.float32),
            pltpu.SemaphoreType.DMA((chunks,)),
        ],
        compiler_params=pltpu.CompilerParams(vmem_limit_bytes=52 * 1024 * 1024),
    )(count, live_tiles, ratings, user_fac, user_acc, held_pair)


CHUNKS = 4


def sum_kernel(axes, x_ref, out_ref, *scratch):
    barrier = pltpu.get_barrier_semaphore()
    peers = 0
    for axis, count in axes:
        me = lax.axis_index(axis)
        for k in range(1, count):
            pl.semaphore_signal(
                barrier, inc=1, device_id={axis: lax.rem(me + k, count)}, device_id_type=pl.DeviceIdType.MESH
            )
        peers += count - 1
    pl.semaphore_wait(barrier, peers)
    value = x_ref[...]
    for (axis, count), at in zip(axes, range(0, len(scratch), 3)):
        slots, send_sems, recv_sems = scratch[at : at + 3]
        me = lax.axis_index(axis)
        slots[0] = value
        copies = []
        for k in range(1, count):
            copy = pltpu.make_async_remote_copy(
                src_ref=slots.at[0],
                dst_ref=slots.at[k],
                send_sem=send_sems.at[k],
                recv_sem=recv_sems.at[k],
                device_id={axis: lax.rem(me + k, count)},
                device_id_type=pl.DeviceIdType.MESH,
            )
            copy.start()
            copies.append(copy)
        for copy in copies:
            copy.wait()
        value = slots[me]
        for source in range(1, count):
            value = value + slots[lax.rem(me - source + count, count)]
    out_ref[...] = value


def summed_everywhere(sums):
    axes = [(axis, lax.axis_size(axis)) for axis in ("col", "row")]
    scratch = []
    for axis, count in axes:
        scratch += [
            pltpu.VMEM((count,) + sums.shape, sums.dtype),
            pltpu.SemaphoreType.DMA((count,)),
            pltpu.SemaphoreType.DMA((count,)),
        ]
    vmem = pl.BlockSpec(memory_space=pltpu.VMEM)
    return pl.pallas_call(
        functools.partial(sum_kernel, axes),
        out_shape=jax.ShapeDtypeStruct(sums.shape, sums.dtype),
        in_specs=[vmem],
        out_specs=vmem,
        scratch_shapes=scratch,
        compiler_params=pltpu.CompilerParams(collective_id=0, has_side_effects=True),
    )(sums)


def segment_plan(group_size, own_tiles):
    total = group_size * own_tiles
    low = [m if m < group_size - 1 else total - 2 * own_tiles for m in range(group_size)]
    high = [total - (group_size - 1 - m) if m else 2 * own_tiles for m in range(group_size)]
    segments = []
    for step in range(1 - group_size, group_size):
        first, last, pairs = own_tiles, 0, []
        for m in range(group_size):
            home = m + step
            if 0 <= home < group_size:
                begin = max(low[m], home * own_tiles) - home * own_tiles
                end = min(high[m], (home + 1) * own_tiles) - home * own_tiles
                if begin < end:
                    first, last = min(first, begin), max(last, end)
                    pairs.append((home, m))
        if step == 0:
            first, last = 0, own_tiles
        if pairs:
            segments.append((step, first, last, pairs))
    return segments


def fetched(own, segments, tile_size, window, rows):
    parts = []
    for step, first, last, pairs in segments:
        part = own[first * tile_size : last * tile_size]
        parts.append(lax.ppermute(part, "col", pairs) if step else part)
    parts.append(jnp.zeros((rows, own.shape[1]), own.dtype))
    return lax.dynamic_slice_in_dim(jnp.concatenate(parts, axis=0), window, rows, 0)


def returned(kept, segments, tile_size, window):
    lengths = [(last - first) * tile_size for step, first, last, pairs in segments]
    frame = jnp.zeros((sum(lengths) + kept.shape[0], kept.shape[1]), kept.dtype)
    frame = lax.dynamic_update_slice_in_dim(frame, kept, window, 0)
    own_rows = [length for length, segment in zip(lengths, segments) if segment[0] == 0][0]
    total, at = None, 0
    for length, (step, first, last, pairs) in zip(lengths, segments):
        part = frame[at : at + length]
        at += length
        if step:
            part = lax.ppermute(part, "col", [(m, home) for home, m in pairs])
        part = jnp.pad(part, ((first * tile_size, own_rows - last * tile_size), (0, 0)))
        total = part if total is None else total + part
    return total


def on_device(ratings, tile_mask, tile_counts, users, user_accum, items, item_accum):
    strata_count = ratings.shape[0]
    slot_count = tile_mask.shape[1]
    tile_size = ratings.shape[1] // slot_count
    group_size = lax.axis_size("col")
    member = lax.axis_index("col")
    arrived_rows = users.shape[0]
    group_counts = lax.dynamic_slice_in_dim(
        tile_counts, lax.axis_index("row") * group_size, group_size
    )
    ranks = jnp.arange(group_size, dtype=jnp.int32)
    start_tile = jnp.sum(jnp.where(ranks < member, group_counts, 0))
    own_count = jnp.sum(jnp.where(ranks == member, group_counts, 0))
    valid = (jnp.arange(slot_count, dtype=jnp.int32) < own_count).astype(jnp.float32)
    pad_rows = slot_count * tile_size
    segments = segment_plan(group_size, arrived_rows // tile_size)
    ahead = -min(step * (arrived_rows // tile_size) + first for step, first, last, pairs in segments)
    window = (start_tile - member * (arrived_rows // tile_size) + ahead) * tile_size
    row_valid = jnp.repeat(valid, tile_size)[:, None] > 0.5
    user_fac = jnp.where(row_valid, fetched(users, segments, tile_size, window, pad_rows), 0.0)
    user_acc = jnp.where(row_valid, fetched(user_accum, segments, tile_size, window, pad_rows), 1.0)
    held_pair = jnp.stack([items, item_accum])
    live_all = tile_mask.astype(jnp.float32) * valid[:, None]
    sq_list = []
    for stratum in range(strata_count):
        user_fac, user_acc, held_pair, squares = run_stratum(
            stratum, own_count[None], live_all[stratum], ratings, user_fac, user_acc, held_pair
        )
        sq_list.append(jnp.sum(squares))
        if stratum + 1 < strata_count:
            held_pair = passed_along(held_pair, ("row", "col"), 1)
    observed = jnp.sum(live_all, axis=(1, 2)) * float(tile_size * tile_size)
    sums = jnp.concatenate([jnp.stack(sq_list), observed])
    sums = jnp.broadcast_to(jnp.pad(sums, (0, items.shape[1] - sums.shape[0]))[None, :], (8, items.shape[1]))
    totals = summed_everywhere(sums)[0]
    total_error, total_count = totals[:strata_count], totals[strata_count : 2 * strata_count]
    losses = total_error / total_count
    users_new = returned(jnp.where(row_valid, user_fac, 0.0), segments, tile_size, window)
    accum_new = returned(jnp.where(row_valid, user_acc, 0.0), segments, tile_size, window)
    return (users_new, accum_new, held_pair[0], held_pair[1], losses)


def solution(mesh):
    return jax.shard_map(
        on_device,
        mesh=mesh,
        in_specs=(
            P(None, ("row", "col"), None),
            P(None, ("row", "col"), None),
            P(),
            P(("row", "col"), None),
            P(("row", "col"), None),
            P(("row", "col"), None),
            P(("row", "col"), None),
        ),
        out_specs=(
            P(("row", "col"), None),
            P(("row", "col"), None),
            P(("row", "col"), None),
            P(("row", "col"), None),
            P(),
        ),
        check_vma=False,
    )
```
